32 devices in a mesh: section: 4 (over x, core), dp: 8 (over z, y).
Axes of the slice: x: 2, y: 2, z: 4, core: 2. Of those that a mesh axis runs over, the one named last changes fastest.
Arguments:
- x_enc: bfloat16 [2, 512, 2048], P(None, 'dp'), may hold values from -6 to 6
- x_dec: bfloat16 [2, 512, 2048], P(None, 'dp'), may hold values from -6 to 6
- d_out: bfloat16 [2, 512, 2048], P(None, 'dp'), may hold values from -6 to 6
- lengths: int32 [2, 8], P(None, 'dp'), may hold values from 16 to 64, as said below
- w_query: bfloat16 [4, 2048, 2048], P('section', 'dp'), may hold values from -0.125 to 0.125
- gain: bfloat16 [4, 2048], P('section', 'dp'), may hold values from 0.5 to 1.5
Outputs:
- section_out: bfloat16 [4, 2, 512, 2048], P('section', None, 'dp')
- d_inputs: bfloat16 [4, 2, 512, 2048], P('section', None, 'dp')
- grad_query: float32 [4, 2048, 2048], P('section', 'dp')
- grad_gain: float32 [4, 2048], P('section', 'dp')
The draws below stay inside these ranges and needn't reach their ends.
Inputs may be any that keep to these rules, and one draw needn't show every extreme that they name: `lengths`: each length is 16 to 64; both ends are taken by some sequence.
All inputs are finite; a program needn't handle non-finite values.
Results may differ from the reference program's by a relative error of at most 0.025.
Values may be sent and summed in bfloat16 or wider, within the bound.
A program may use at most 128 MiB of HBM per device.

```python
import jax
import jax.numpy as jnp
from jax import lax

D = 2048
HEAD = 256
MB = 2
SEQ = 64
BATCH = 8
SECTIONS = 4
N_SECTION = 4


def draw_lengths(key, part):
    key = jax.random.fold_in(key, 5)
    drawn = jax.random.randint(key, (MB, BATCH), SEQ // 4, SEQ + 1)
    drawn = drawn.at[0, 0].set(SEQ)
    drawn = drawn.at[MB - 1, BATCH - 1].set(SEQ // 4)
    return drawn.astype(jnp.int32)


def level_of(rng, shape, pieces, low, high):
    level, own = 1.0, jax.random.fold_in(rng, 6)
    for dim, shards_of in pieces:
        heights = jnp.exp(jax.random.uniform(jax.random.fold_in(own, dim), (shards_of,), jnp.float32, low / len(pieces), high / len(pieces)))
        level = level * jnp.repeat(heights, shape[dim] // shards_of).reshape([-1 if axis == dim else 1 for axis in range(len(shape))])
    return level


def bell_draw(key, shape, spread, reach, split=(), kind=jnp.bfloat16):
    result = jax.random.normal(key, shape, jnp.float32) * spread
    if len(split) > 0:
        result = level_of(key, shape, split, -0.22, 0.18) * result
    return jnp.clip(result, min=-reach, max=reach).astype(kind)


def setup_inputs(seed: int = 0) -> dict:
    seeds = jax.random.split(jax.random.key(seed), 7)
    return {
        "x_enc": bell_draw(seeds[0], (MB, BATCH * SEQ, D), 1.0, 6.0, ((1, 8),)),
        "x_dec": bell_draw(seeds[1], (MB, BATCH * SEQ, D), 1.0, 6.0, ((1, 8),)),
        "d_out": bell_draw(seeds[2], (MB, BATCH * SEQ, D), 1.0, 6.0, ((1, 8),)),
        "lengths": draw_lengths(jax.random.fold_in(seeds[6], 71), 0),
        "w_query": bell_draw(seeds[4], (SECTIONS, D, D), D ** -0.5, 0.125, ((0, 4), (1, 8))),
        "gain": jnp.clip(1.0 + 0.1 * jax.random.normal(seeds[5], (SECTIONS, D), jnp.float32), 0.5, 1.5).astype(jnp.bfloat16),
    }


norm_eps = 1e-06
mix_scale = 4.0

def contract(left, right, left_dim, right_dim):
    return lax.dot_general(left, right, (((left_dim,), (right_dim,)), ((), ())), preferred_element_type=jnp.float32)

def normed(values, gain_row):
    squares = lax.optimization_barrier(jnp.mean(values * values, axis=-1, keepdims=True))
    return (values * lax.rsqrt(squares + norm_eps) * gain_row).astype(jnp.bfloat16)

def prepare(inputs_f32, source_f32, gain_f32):
    return (normed(inputs_f32, gain_f32), normed(source_f32, gain_f32))

def attend(query, keys, source):
    row_count, features = query.shape
    heads = features // HEAD
    score_scale = HEAD ** (-0.5)
    query_heads = query.astype(jnp.float32).reshape(row_count, heads, HEAD)
    key_heads = keys.astype(jnp.float32).reshape(-1, heads, HEAD)
    value_heads = source.astype(jnp.float32).reshape(-1, heads, HEAD)
    scores = jnp.einsum('qhd,khd->hqk', query_heads, key_heads) * score_scale
    weights = jnp.exp(scores)
    probs = (weights / lax.optimization_barrier(jnp.sum(weights, axis=-1, keepdims=True))).astype(jnp.bfloat16)
    mixed = jnp.einsum('hqk,khd->qhd', probs.astype(jnp.float32), value_heads)
    return mixed.reshape(row_count, features).astype(jnp.bfloat16)

def forward_layer(layer_input, source, w_query, gain_row):
    normed_query, keys = prepare(layer_input.astype(jnp.float32), source.astype(jnp.float32), gain_row.astype(jnp.float32))
    query = jnp.dot(normed_query, w_query, preferred_element_type=jnp.float32).astype(jnp.bfloat16)
    mixed = attend(query, keys, source)
    return (layer_input.astype(jnp.float32) + mix_scale * mixed.astype(jnp.float32)).astype(jnp.bfloat16)

def backward_layer(layer_input, source, d_result, w_query, gain_row):
    (normed_query, keys), prep_back = jax.vjp(prepare, layer_input.astype(jnp.float32), source.astype(jnp.float32), gain_row.astype(jnp.float32))
    query = jnp.dot(normed_query, w_query, preferred_element_type=jnp.float32).astype(jnp.bfloat16)
    mixed, attend_back = jax.vjp(attend, query, keys, source)
    d_mixed = (mix_scale * d_result.astype(jnp.float32)).astype(jnp.bfloat16)
    d_query, d_keys, d_values = attend_back(d_mixed)
    d_normed = contract(d_query, w_query, 1, 1).astype(jnp.bfloat16)
    d_input, d_source, d_gain = prep_back((d_normed, d_keys))
    d_input = d_input + d_result.astype(jnp.float32)
    d_source = d_source + d_values.astype(jnp.float32)
    return (d_input, d_source, d_gain, normed_query, d_query)

def rounded_sum(total, partial_value):
    return total + lax.optimization_barrier(partial_value.astype(jnp.bfloat16)).astype(jnp.float32)

def reference(x_enc, x_dec, d_out, lengths, w_query, gain):

    def per_sequence(totals, sequence):
        enc_rows, dec_rows, out_rows, limits = sequence
        inputs_of = [[None] * MB for section_num in range(N_SECTION)]
        results = [[None] * MB for section_num in range(N_SECTION)]
        for batch_slot in range(MB):
            inputs_of[0][batch_slot] = enc_rows[batch_slot]
            results[0][batch_slot] = forward_layer(enc_rows[batch_slot], enc_rows[batch_slot], w_query[0], gain[0])
        for section_num in range(1, N_SECTION):
            for batch_slot in range(MB):
                if section_num == 1:
                    layer_input = (dec_rows[batch_slot].astype(jnp.float32) + results[0][batch_slot].astype(jnp.float32)).astype(jnp.bfloat16)
                else:
                    layer_input = results[section_num - 1][batch_slot]
                inputs_of[section_num][batch_slot] = layer_input
                results[section_num][batch_slot] = forward_layer(layer_input, results[0][batch_slot], w_query[section_num], gain[section_num])
        row_index = lax.broadcasted_iota(jnp.int32, (SEQ, 1), 0)
        d_memory = [jnp.zeros((SEQ, D), jnp.float32) for batch_slot in range(MB)]
        d_inputs = [[None] * MB for section_num in range(N_SECTION)]
        saved = [[[], []] for section_num in range(N_SECTION)]
        gain_terms = [jnp.zeros((D,), jnp.float32) for section_num in range(N_SECTION)]
        for section_num in range(N_SECTION - 1, 0, -1):
            for batch_slot in range(MB):
                if section_num == N_SECTION - 1:
                    d_result = jnp.where(row_index < limits[batch_slot], out_rows[batch_slot], jnp.zeros_like(out_rows[batch_slot]))
                else:
                    d_result = d_inputs[section_num + 1][batch_slot]
                parts = backward_layer(inputs_of[section_num][batch_slot], results[0][batch_slot], d_result, w_query[section_num], gain[section_num])
                d_inputs[section_num][batch_slot] = parts[0].astype(jnp.bfloat16)
                d_memory[batch_slot] = d_memory[batch_slot] + parts[1]
                if section_num == 1:
                    d_memory[batch_slot] = d_memory[batch_slot] + lax.optimization_barrier(d_inputs[1][batch_slot]).astype(jnp.float32)
                gain_terms[section_num] = gain_terms[section_num] + parts[2]
                saved[section_num][0].append(parts[3])
                saved[section_num][1].append(parts[4])
        for batch_slot in range(MB):
            d_result = d_memory[batch_slot].astype(jnp.bfloat16)
            parts = backward_layer(inputs_of[0][batch_slot], inputs_of[0][batch_slot], d_result, w_query[0], gain[0])
            d_inputs[0][batch_slot] = (parts[0] + parts[1]).astype(jnp.bfloat16)
            gain_terms[0] = gain_terms[0] + parts[2]
            saved[0][0].append(parts[3])
            saved[0][1].append(parts[4])
        query_parts = []
        for section_num in range(N_SECTION):
            flat = [jnp.stack(group).reshape(MB * SEQ, D) for group in saved[section_num]]
            query_parts.append(contract(flat[0], flat[1], 0, 0))
        total_query, total_gain = totals
        total_query = rounded_sum(total_query, jnp.stack(query_parts))
        total_gain = rounded_sum(total_gain, jnp.stack(gain_terms))
        outputs = jnp.stack([jnp.stack(row) for row in results])
        cotangents = jnp.stack([jnp.stack(row) for row in d_inputs])
        return ((total_query, total_gain), (outputs, cotangents))

    def by_sequence(array):
        return array.reshape(MB, BATCH, SEQ, D).transpose(1, 0, 2, 3)
    start = (jnp.zeros((N_SECTION, D, D), jnp.float32), jnp.zeros((N_SECTION, D), jnp.float32))
    totals, stacked = lax.scan(per_sequence, start, (by_sequence(x_enc), by_sequence(x_dec), by_sequence(d_out), lengths.T))
    section_out = stacked[0].transpose(1, 2, 0, 3, 4).reshape(N_SECTION, MB, BATCH * SEQ, D)
    d_inputs = stacked[1].transpose(1, 2, 0, 3, 4).reshape(N_SECTION, MB, BATCH * SEQ, D)
    return (section_out, d_inputs, totals[0], totals[1])
```

```python
import functools

import jax
import jax.numpy as jnp
from jax import lax
from jax.experimental import pallas as pl
from jax.experimental.pallas import tpu as pltpu
from jax.sharding import PartitionSpec as P

HEAD = 256
norm_eps = 1e-06
mix_scale = 4.0
TAIL = 128
F32, BF16 = jnp.float32, jnp.bfloat16


def dot(left, right, left_dim, right_dim):
    return lax.dot_general(
        left, right, (((left_dim,), (right_dim,)), ((), ())), preferred_element_type=F32
    )


def inv_norm(chunks, features):
    total = sum(jnp.sum(c * c, axis=-1, keepdims=True) for c in chunks)
    return lax.rsqrt(total * (1.0 / features) + norm_eps)


def softmax_parts(query, keys):
    weights = jnp.exp(dot(query, keys, 1, 1) * HEAD ** (-0.5))
    return weights / jnp.sum(weights, axis=-1, keepdims=True)


def cascade_kernel(
    n, micro, x_enc, x_dec, d_last, weights, gain,
    out_ref, din_ref, nq_ref, dq_ref, dg_ref,
    y_buf, x_one, p_send, p_recv, d_own, d_recv, q_buf,
    y_ss, y_rs, p_ss, p_rs, d_ss, d_rs,
):
    rows, features = x_enc.shape
    seq = rows // micro
    width = features // n
    heads = width // HEAD
    me = lax.axis_index("section")
    mine = pl.ds(pl.multiple_of(me * width, width), width)
    peers = [lax.rem(me + k, n) for k in range(1, n)]
    behind = [lax.rem(me + n - k, n) for k in range(1, n)]

    def cols(j):
        return slice(j * width, (j + 1) * width)

    barrier = pltpu.get_barrier_semaphore()
    for peer in peers:
        pl.semaphore_signal(
            barrier, inc=1, device_id={"section": peer}, device_id_type=pl.DeviceIdType.MESH
        )
    pl.semaphore_wait(barrier, n - 1)

    def push(src, dst, send, recv, peer):
        copy = pltpu.make_async_remote_copy(
            src_ref=src, dst_ref=dst, send_sem=send, recv_sem=recv,
            device_id={"section": peer}, device_id_type=pl.DeviceIdType.MESH,
        )
        copy.start()
        return copy

    pending = []

    def layer_in(layer, j):
        if layer == 0:
            return x_enc[:, cols(j)].astype(F32)
        if layer == 1:
            return x_one[j].astype(F32)
        return y_buf[layer - 1, j].astype(F32)

    def own_in(layer):
        if layer == 0:
            return x_enc[:, mine]
        if layer == 1:
            return x_one[me]
        return y_buf[layer - 1, me]

    def own_source(layer):
        return x_enc[:, mine] if layer == 0 else y_buf[0, me]

    inv_in = [None] * n
    inv_src = [None] * n

    def keys_of(layer, source):
        return (source.astype(F32) * inv_src[layer] * gain[layer : layer + 1, mine].astype(F32)).astype(BF16)

    for layer in range(n):
        if layer == 1:
            for j in range(n):
                x_one[j] = (x_dec[:, cols(j)].astype(F32) + y_buf[0, j].astype(F32)).astype(BF16)
            inv_memory = inv_norm([y_buf[0, j].astype(F32) for j in range(n)], features)
        inv = inv_norm([layer_in(layer, j) for j in range(n)], features)
        inv_in[layer] = inv
        inv_src[layer] = inv if layer == 0 else inv_memory
        query = jnp.zeros((rows, width), F32)
        for j in range(n):
            part = (layer_in(layer, j) * inv * gain[layer : layer + 1, cols(j)].astype(F32)).astype(BF16)
            nq_ref[layer, :, cols(j)] = part
            query = query + dot(part, weights[layer, cols(j), :], 1, 0)
        query = query.astype(BF16)
        q_buf[layer] = query
        source = own_source(layer)
        keys = keys_of(layer, source)
        bands = []
        for m in range(micro):
            r = slice(m * seq, (m + 1) * seq)
            pieces = []
            for h in range(heads):
                c = slice(h * HEAD, (h + 1) * HEAD)
                probs = softmax_parts(query[r, c], keys[r, c]).astype(BF16)
                pieces.append(dot(probs, source[r, c], 1, 0))
            bands.append(jnp.concatenate(pieces, axis=1))
        mixed = jnp.concatenate(bands, axis=0).astype(BF16).astype(F32)
        y_buf[layer, me] = (own_in(layer).astype(F32) + mix_scale * mixed).astype(BF16)
        copies = [
            push(y_buf.at[layer, me], y_buf.at[layer, me], y_ss.at[layer, k], y_rs.at[layer, k], peer)
            for k, peer in enumerate(peers)
        ]
        for copy in copies:
            copy.wait_recv()
        pending += copies

    for j in range(n):
        out_ref[:, cols(j)] = y_buf[me, j]

    d_result = d_last[:, mine]
    d_memory = jnp.zeros((rows, width), F32)
    for layer in range(n - 1, -1, -1):
        g = gain[layer : layer + 1, mine].astype(F32)
        source = own_source(layer)
        keys = keys_of(layer, source)
        query = q_buf[layer]
        d_mixed = (mix_scale * d_result.astype(F32)).astype(BF16)
        dq_bands, dk_bands, dv_bands = [], [], []
        for m in range(micro):
            r = slice(m * seq, (m + 1) * seq)
            dq_p, dk_p, dv_p = [], [], []
            for h in range(heads):
                c = slice(h * HEAD, (h + 1) * HEAD)
                probs = softmax_parts(query[r, c], keys[r, c])
                d_probs = dot(d_mixed[r, c], source[r, c], 1, 1).astype(BF16).astype(F32)
                dv_p.append(dot(probs.astype(BF16), d_mixed[r, c], 0, 0))
                inner = jnp.sum(d_probs * probs, axis=-1, keepdims=True)
                d_scores = (probs * (d_probs - inner) * HEAD ** (-0.5)).astype(BF16)
                dq_p.append(dot(d_scores, keys[r, c], 1, 0))
                dk_p.append(dot(d_scores, query[r, c], 0, 0))
            dq_bands.append(jnp.concatenate(dq_p, axis=1))
            dk_bands.append(jnp.concatenate(dk_p, axis=1))
            dv_bands.append(jnp.concatenate(dv_p, axis=1))
        d_query = jnp.concatenate(dq_bands, axis=0).astype(BF16)
        d_keys = jnp.concatenate(dk_bands, axis=0).astype(BF16).astype(F32)
        d_values = jnp.concatenate(dv_bands, axis=0).astype(BF16).astype(F32)
        dq_ref[layer] = d_query
        q_sum = jnp.sum(d_query.astype(F32) * query.astype(F32), axis=-1, keepdims=True)
        k_sum = jnp.sum(d_keys * keys.astype(F32), axis=-1, keepdims=True)
        q_hi = q_sum.astype(BF16).astype(F32)
        k_hi = k_sum.astype(BF16).astype(F32)
        lane = lax.broadcasted_iota(jnp.int32, (rows, TAIL), 1)
        tail = jnp.where(
            lane == 0, q_hi, jnp.where(lane == 1, q_sum - q_hi, jnp.where(lane == 2, k_hi, k_sum - k_hi))
        ).astype(BF16)
        for j in range(n):
            p_send[layer, j, :, :width] = dot(d_query, weights[layer, cols(j), :], 1, 1).astype(BF16)
            p_send[layer, j, :, width:] = tail
        copies = [
            push(p_send.at[layer, peer], p_recv.at[layer, me], p_ss.at[layer, k], p_rs.at[layer, k], peer)
            for k, peer in enumerate(peers)
        ]
        for copy in copies:
            copy.wait_recv()
        pending += copies
        blocks = [p_send[layer, me]] + [p_recv[layer, b] for b in behind]
        d_normed = sum(b[:, :width].astype(F32) for b in blocks).astype(BF16).astype(F32)
        sums = sum(b[:, width:].astype(F32) for b in blocks)
        q_tot = sums[:, 0:1] + sums[:, 1:2]
        k_tot = sums[:, 2:3] + sums[:, 3:4]
        inv, inv_m = inv_in[layer], inv_src[layer]
        x_own = own_in(layer).astype(F32)
        s_own = source.astype(F32)
        d_input = d_result.astype(F32) + inv * (g * d_normed) - x_own * (inv * inv * q_tot * (1.0 / features))
        d_source = inv_m * (g * d_keys) - s_own * (inv_m * inv_m * k_tot * (1.0 / features)) + d_values
        dg_ref[layer : layer + 1, :] = jnp.sum(
            x_own * inv * d_normed + s_own * inv_m * d_keys, axis=0, keepdims=True
        )
        if layer == 0:
            d_own[0] = (d_input + d_source).astype(BF16)
        else:
            d_result = d_input.astype(BF16)
            d_own[layer] = d_result
            d_memory = d_memory + d_source
            if layer == 1:
                d_result = (d_memory + d_result.astype(F32)).astype(BF16)

    copies = [
        push(d_own.at[peer], d_recv.at[me], d_ss.at[k], d_rs.at[k], peer) for k, peer in enumerate(peers)
    ]
    d_recv[me] = d_own[me]
    for copy in copies:
        copy.wait_recv()
    for j in range(n):
        din_ref[:, cols(j)] = d_recv[j]
    for copy in pending + copies:
        copy.wait_send()


def cascade(n, micro, x_enc, x_dec, d_last, weights, gain):
    rows, features = x_enc.shape
    width = features // n
    vmem = pl.BlockSpec(memory_space=pltpu.VMEM)
    sds = jax.ShapeDtypeStruct
    dma = pltpu.SemaphoreType.DMA
    return pl.pallas_call(
        functools.partial(cascade_kernel, n, micro),
        out_shape=(
            sds((rows, features), BF16),
            sds((rows, features), BF16),
            sds((n, rows, features), BF16),
            sds((n, rows, width), BF16),
            sds((n, width), F32),
        ),
        in_specs=[vmem] * 5,
        out_specs=[vmem] * 5,
        scratch_shapes=[
            pltpu.VMEM((n, n, rows, width), BF16),
            pltpu.VMEM((n, rows, width), BF16),
            pltpu.VMEM((n, n, rows, width + TAIL), BF16),
            pltpu.VMEM((n, n, rows, width + TAIL), BF16),
            pltpu.VMEM((n, rows, width), BF16),
            pltpu.VMEM((n, rows, width), BF16),
            pltpu.VMEM((n, rows, width), BF16),
            dma((n, n - 1)), dma((n, n - 1)),
            dma((n, n - 1)), dma((n, n - 1)),
            dma((n - 1,)), dma((n - 1,)),
        ],
        compiler_params=pltpu.CompilerParams(
            collective_id=0, has_side_effects=True, vmem_limit_bytes=56 * 1024 * 1024
        ),
    )(x_enc, x_dec, d_last, weights, gain)


def shards(x_enc, x_dec, d_out, lengths, w_query, gain):
    n = lax.axis_size("section")
    micro, seq, features = x_enc.shape
    rows = micro * seq
    width = features // n
    row_index = lax.broadcasted_iota(jnp.int32, (micro, seq, 1), 1)
    d_last = jnp.where(row_index < lengths[:, :, None], d_out, jnp.zeros_like(d_out))
    split = w_query[0].reshape(-1, n, width).transpose(1, 0, 2)
    own = lax.all_to_all(split, "section", 0, 0, tiled=True)
    weights = lax.all_gather(own, "dp", axis=1, tiled=True)
    full_gain = lax.all_gather(lax.all_gather(gain, "dp", axis=1, tiled=True), "section", axis=0, tiled=True)
    out, d_in, normed, d_query, d_gain = cascade(
        n, micro, x_enc.reshape(rows, features), x_dec.reshape(rows, features),
        d_last.reshape(rows, features), weights, full_gain,
    )
    part = jnp.einsum("lrf,lrc->lfc", normed, d_query, preferred_element_type=F32).astype(BF16)
    part = lax.psum_scatter(part, "dp", scatter_dimension=1, tiled=True)
    grad = lax.all_to_all(part, "section", 0, 0, tiled=True)
    grad = grad.transpose(1, 0, 2).reshape(1, -1, features).astype(F32)
    gains = lax.psum_scatter(
        lax.all_to_all(d_gain.astype(BF16), "section", 0, 0, tiled=True).reshape(1, features),
        "dp", scatter_dimension=1, tiled=True,
    ).astype(F32)
    return (
        out.reshape(1, micro, seq, features),
        d_in.reshape(1, micro, seq, features),
        grad,
        gains,
    )


def solution(mesh):
    in_specs = (
        P(None, "dp", None), P(None, "dp", None), P(None, "dp", None),
        P(None, "dp"), P("section", "dp", None), P("section", "dp"),
    )
    out_specs = (
        P("section", None, "dp", None), P("section", None, "dp", None),
        P("section", "dp", None), P("section", "dp"),
    )
    return jax.shard_map(shards, mesh=mesh, in_specs=in_specs, out_specs=out_specs, check_vma=False)
```

```python
import functools

import jax
import jax.numpy as jnp
from jax import lax
from jax.experimental import pallas as pl
from jax.experimental.pallas import tpu as pltpu
from jax.sharding import PartitionSpec as P

HEAD = 256
norm_eps = 1e-06
mix_scale = 4.0
TAIL = 128
F32, BF16 = jnp.float32, jnp.bfloat16


def dot(left, right, left_dim, right_dim):
    return lax.dot_general(
        left, right, (((left_dim,), (right_dim,)), ((), ())), preferred_element_type=F32
    )


def inv_norm(chunks, features):
    total = sum(jnp.sum(c * c, axis=-1, keepdims=True) for c in chunks)
    return lax.rsqrt(total * (1.0 / features) + norm_eps)


def softmax_parts(query, keys):
    weights = jnp.exp(dot(query, keys, 1, 1) * HEAD ** (-0.5))
    return weights / jnp.sum(weights, axis=-1, keepdims=True)


MESH = pl.DeviceIdType.MESH
PAD = 16


class Spread:
    def __init__(self, buf, count, sems):
        self.buf, self.count = buf, count
        self.chain_s, self.chain_r, self.pair_s, self.pair_r = sems
        here = lax.axis_index("dp")
        self.place, self.side = here // 2, lax.rem(here, 2)

    def copy(self, layer, place, side, send, recv, to_place, to_side):
        block = self.buf.at[layer, place * 2 + side]
        return pltpu.make_async_remote_copy(
            src_ref=block, dst_ref=block, send_sem=send, recv_sem=recv,
            device_id={"dp": to_place * 2 + to_side}, device_id_type=MESH,
        )

    def chain(self, layer, step, way):
        sign = 1 if way == 0 else -1
        return self.copy(
            layer, self.place - sign * step, self.side,
            self.chain_s.at[way, layer, step], self.chain_r.at[way, layer, step],
            self.place + sign, self.side,
        )

    def pair(self, layer, step, way, side):
        sign = 1 if way == 0 else -1
        slot = step if way == 0 else self.count - 1 + step
        return self.copy(
            layer, self.place - sign * step, side,
            self.pair_s.at[layer, slot], self.pair_r.at[layer, slot], self.place, 1 - self.side,
        )

    def holds(self, step, way):
        return self.place >= step if way == 0 else self.place + step < self.count

    def passes(self, step, way):
        end = self.place + 1 < self.count if way == 0 else self.place >= 1
        return jnp.logical_and(self.holds(step, way), end)

    def arrived(self, layer, step, way):
        sign = 1 if way == 0 else -1
        return self.copy(
            layer, self.place - sign * step, self.side,
            self.chain_s.at[way, layer, step - 1], self.chain_r.at[way, layer, step - 1],
            self.place + sign, self.side,
        )

    def pump(self, layer, step):
        for way in (0, 1):
            if step > 0:
                @pl.when(self.holds(step, way))
                def _():
                    self.arrived(layer, step, way).wait_recv()

            if step < self.count - 1:
                @pl.when(self.passes(step, way))
                def _():
                    self.chain(layer, step, way).start()

            if step == 0:
                if way == 0:
                    self.pair(layer, 0, 0, self.side).start()
            else:
                @pl.when(self.holds(step, way))
                def _():
                    self.pair(layer, step, way, self.side).start()

    def finish(self, layer):
        self.pair(layer, 0, 0, 1 - self.side).wait_recv()
        for step in range(1, self.count):
            for way in (0, 1):
                @pl.when(self.holds(step, way))
                def _():
                    self.pair(layer, step, way, 1 - self.side).wait_recv()

    def drain(self, layer):
        self.pair(layer, 0, 0, self.side).wait_send()
        for step in range(self.count):
            for way in (0, 1):
                if step < self.count - 1:
                    @pl.when(self.passes(step, way))
                    def _():
                        self.chain(layer, step, way).wait_send()

                if step > 0:
                    @pl.when(self.holds(step, way))
                    def _():
                        self.pair(layer, step, way, self.side).wait_send()


def cascade_kernel(
    n, nd, micro, x_enc, x_dec, d_last, payload,
    out_ref, din_ref, grad_ref, dg_ref,
    weights, dq_all, nq_own, nq_all, gain, y_buf, x_one, p_send, p_recv, d_own, d_recv, q_buf, g_send, g_recv,
    y_ss, y_rs, p_ss, p_rs, d_ss, d_rs, g_ss, g_rs, a_ss, a_rs, n_ss, n_rs,
    wz_s, wz_r, wy_s, wy_r, qz_s, qz_r, qy_s, qy_r,
):
    rows, features = x_enc.shape
    seq = rows // micro
    width = features // n
    depth = features // nd
    share = width // depth
    half = nd // 2
    heads = width // HEAD
    me = lax.axis_index("section")
    here = lax.axis_index("dp")
    mine = pl.ds(pl.multiple_of(me * width, width), width)
    peers = [lax.rem(me + k, n) for k in range(1, n)]
    behind = [lax.rem(me + n - k, n) for k in range(1, n)]
    dp_peers = [lax.rem(here + k, nd) for k in range(1, nd)]

    def cols(j):
        return slice(j * width, (j + 1) * width)

    barrier = pltpu.get_barrier_semaphore()
    for peer in peers:
        pl.semaphore_signal(barrier, inc=1, device_id={"section": peer}, device_id_type=MESH)
    for peer in dp_peers:
        pl.semaphore_signal(barrier, inc=1, device_id={"dp": peer}, device_id_type=MESH)
    pl.semaphore_wait(barrier, n - 1 + nd - 1)

    def describe(src, dst, send, recv, peer, axis="section"):
        return pltpu.make_async_remote_copy(
            src_ref=src, dst_ref=dst, send_sem=send, recv_sem=recv,
            device_id={axis: peer}, device_id_type=MESH,
        )

    def push(*args):
        copy = describe(*args)
        copy.start()
        return copy

    pending = []
    w_spread = Spread(weights, half, (wz_s, wz_r, wy_s, wy_r))
    q_spread = Spread(dq_all, half, (qz_s, qz_r, qy_s, qy_r))

    for k, peer in enumerate(peers):
        pending.append(
            push(payload.at[peer], weights.at[me, here], a_ss.at[k], a_rs.at[me], peer)
        )
    weights[me, here] = payload[me]

    def pump_weights(layer, step):
        if step == 0:
            @pl.when(me != layer)
            def _():
                describe(
                    payload.at[me], weights.at[layer, here], a_ss.at[0], a_rs.at[layer], peers[0]
                ).wait_recv()

        w_spread.pump(layer, step)

    def weight_clock(clock):
        for layer in range(n):
            if 0 <= clock - layer < half:
                pump_weights(layer, clock - layer)

    def layer_in(layer, j):
        if layer == 0:
            return x_enc[:, cols(j)].astype(F32)
        if layer == 1:
            return x_one[j].astype(F32)
        return y_buf[layer - 1, j].astype(F32)

    def own_in(layer):
        if layer == 0:
            return x_enc[:, mine]
        if layer == 1:
            return x_one[me]
        return y_buf[layer - 1, me]

    def own_source(layer):
        return x_enc[:, mine] if layer == 0 else y_buf[0, me]

    inv_in = [None] * n
    inv_src = [None] * n

    def gain_of(layer):
        return gain[layer, me][0:1].astype(F32)

    def keys_of(layer, source):
        return (source.astype(F32) * inv_src[layer] * gain_of(layer)).astype(BF16)

    for clock in range(half):
        weight_clock(clock)

    for layer in range(n):
        if layer == 1:
            for j in range(n):
                x_one[j] = (x_dec[:, cols(j)].astype(F32) + y_buf[0, j].astype(F32)).astype(BF16)
            inv_memory = inv_norm([y_buf[0, j].astype(F32) for j in range(n)], features)
        inv = inv_norm([layer_in(layer, j) for j in range(n)], features)
        inv_in[layer] = inv
        inv_src[layer] = inv if layer == 0 else inv_memory
        weight_clock(half + layer)
        w_spread.finish(layer)
        query = jnp.zeros((rows, width), F32)
        for j in range(n):
            scaled = layer_in(layer, j) * inv
            for i in range(share):
                b = j * share + i
                lanes = slice(i * depth, (i + 1) * depth)
                row = weights[layer, b, depth : depth + PAD, :depth]
                gain[layer, j, :, lanes] = row
                part = (scaled[:, lanes] * row[0:1].astype(F32)).astype(BF16)
                nq_own[layer, b] = part
                query = query + dot(part, weights[layer, b, :depth, :], 1, 0)
        query = query.astype(BF16)
        q_buf[layer] = query
        source = own_source(layer)
        keys = keys_of(layer, source)
        bands = []
        for m in range(micro):
            r = slice(m * seq, (m + 1) * seq)
            pieces = []
            for h in range(heads):
                c = slice(h * HEAD, (h + 1) * HEAD)
                probs = softmax_parts(query[r, c], keys[r, c]).astype(BF16)
                pieces.append(dot(probs, source[r, c], 1, 0))
            bands.append(jnp.concatenate(pieces, axis=1))
        mixed = jnp.concatenate(bands, axis=0).astype(BF16).astype(F32)
        y_buf[layer, me] = (own_in(layer).astype(F32) + mix_scale * mixed).astype(BF16)
        copies = [
            push(y_buf.at[layer, me], y_buf.at[layer, me], y_ss.at[layer, k], y_rs.at[layer, k], peer)
            for k, peer in enumerate(peers)
        ]
        if layer < n - 1:
            for copy in copies:
                copy.wait_recv()
        else:
            last = copies
        pending += copies

    nq_copies = []
    for layer in range(n - 1, -1, -1):
        for k, peer in enumerate(dp_peers):
            nq_copies.append(
                push(
                    nq_own.at[layer, peer], nq_all.at[layer, here],
                    n_ss.at[layer, k], n_rs.at[layer, k], peer, "dp",
                )
            )
        nq_all[layer, here] = nq_own[layer, here]

    def query_clock(clock):
        for i in range(n):
            if 0 <= clock - i < half:
                q_spread.pump(n - 1 - i, clock - i)

    def gradient(layer):
        q_spread.finish(layer)
        i = n - 1 - layer
        for copy in nq_copies[i * (nd - 1) : (i + 1) * (nd - 1)]:
            copy.wait_recv()
        left = nq_all[layer].reshape(nd * rows, depth)
        right = jnp.concatenate([dq_all[layer, b, :rows, :] for b in range(nd)], axis=0)
        g_send[layer, :depth, :] = dot(left, right, 0, 0).astype(BF16)
        total = sum(dq_all[layer, b, rows : rows + PAD, :].astype(F32) for b in range(nd))
        g_send[layer, depth:, :] = total.astype(BF16)
        deliver(g_send, g_recv, g_ss, g_rs, layer)

    def to_layer(buf, landing, send, recv, layer):
        return describe(buf.at[layer], landing.at[me], send.at[layer], recv.at[me], layer)

    def deliver(buf, landing, send, recv, layer):
        @pl.when(me != layer)
        def _():
            to_layer(buf, landing, send, recv, layer).start()

        @pl.when(me == layer)
        def _():
            landing[me] = buf[layer]

    def collect(buf, landing, send, recv):
        for b in behind:
            describe(buf.at[0], landing.at[b], send.at[0], recv.at[b], b).wait_recv()

    d_result = d_last[:, mine]
    d_memory = jnp.zeros((rows, width), F32)
    for layer in range(n - 1, -1, -1):
        g = gain_of(layer)
        source = own_source(layer)
        keys = keys_of(layer, source)
        query = q_buf[layer]
        d_mixed = (mix_scale * d_result.astype(F32)).astype(BF16)
        dq_bands, dk_bands, dv_bands = [], [], []
        for m in range(micro):
            r = slice(m * seq, (m + 1) * seq)
            dq_p, dk_p, dv_p = [], [], []
            for h in range(heads):
                c = slice(h * HEAD, (h + 1) * HEAD)
                probs = softmax_parts(query[r, c], keys[r, c])
                d_probs = dot(d_mixed[r, c], source[r, c], 1, 1).astype(BF16).astype(F32)
                dv_p.append(dot(probs.astype(BF16), d_mixed[r, c], 0, 0))
                inner = jnp.sum(d_probs * probs, axis=-1, keepdims=True)
                d_scores = (probs * (d_probs - inner) * HEAD ** (-0.5)).astype(BF16)
                dq_p.append(dot(d_scores, keys[r, c], 1, 0))
                dk_p.append(dot(d_scores, query[r, c], 0, 0))
            dq_bands.append(jnp.concatenate(dq_p, axis=1))
            dk_bands.append(jnp.concatenate(dk_p, axis=1))
            dv_bands.append(jnp.concatenate(dv_p, axis=1))
        d_query = jnp.concatenate(dq_bands, axis=0).astype(BF16)
        d_keys = jnp.concatenate(dk_bands, axis=0).astype(BF16).astype(F32)
        d_values = jnp.concatenate(dv_bands, axis=0).astype(BF16).astype(F32)
        q_sum = jnp.sum(d_query.astype(F32) * query.astype(F32), axis=-1, keepdims=True)
        k_sum = jnp.sum(d_keys * keys.astype(F32), axis=-1, keepdims=True)
        q_hi = q_sum.astype(BF16).astype(F32)
        k_hi = k_sum.astype(BF16).astype(F32)
        lane = lax.broadcasted_iota(jnp.int32, (rows, TAIL), 1)
        tail = jnp.where(
            lane == 0, q_hi, jnp.where(lane == 1, q_sum - q_hi, jnp.where(lane == 2, k_hi, k_sum - k_hi))
        ).astype(BF16)
        for b in range(nd):
            lanes = slice((b % share) * depth, (b % share + 1) * depth)
            p_send[layer, b // share, :, lanes] = dot(
                d_query, weights[layer, b, :depth, :], 1, 1
            ).astype(BF16)
        for j in range(n):
            p_send[layer, j, :, width:] = tail
        copies = [
            push(p_send.at[layer, peer], p_recv.at[layer, me], p_ss.at[layer, k], p_rs.at[layer, k], peer)
            for k, peer in enumerate(peers)
        ]
        for copy in copies:
            copy.wait_recv()
        pending += copies
        blocks = [p_send[layer, me]] + [p_recv[layer, b] for b in behind]
        d_normed = sum(b[:, :width].astype(F32) for b in blocks).astype(BF16).astype(F32)
        sums = sum(b[:, width:].astype(F32) for b in blocks)
        q_tot = sums[:, 0:1] + sums[:, 1:2]
        k_tot = sums[:, 2:3] + sums[:, 3:4]
        inv, inv_m = inv_in[layer], inv_src[layer]
        x_own = own_in(layer).astype(F32)
        s_own = source.astype(F32)
        d_input = d_result.astype(F32) + inv * (g * d_normed) - x_own * (inv * inv * q_tot * (1.0 / features))
        d_source = inv_m * (g * d_keys) - s_own * (inv_m * inv_m * k_tot * (1.0 / features)) + d_values
        gain_part = jnp.sum(x_own * inv * d_normed + s_own * inv_m * d_keys, axis=0, keepdims=True)
        dq_all[layer, here, :rows, :] = d_query
        dq_all[layer, here, rows:, :] = jnp.broadcast_to(gain_part, (PAD, width)).astype(BF16)
        query_clock(n - 1 - layer)
        if layer == 0:
            d_own[0] = (d_input + d_source).astype(BF16)
        else:
            d_result = d_input.astype(BF16)
            d_own[layer] = d_result
            d_memory = d_memory + d_source
            if layer == 1:
                d_result = (d_memory + d_result.astype(F32)).astype(BF16)
        deliver(d_own, d_recv, d_ss, d_rs, layer)

    for copy in last:
        copy.wait_recv()
    for j in range(n):
        out_ref[:, cols(j)] = y_buf[me, j]
    done = 0
    for clock in range(n, n + half):
        query_clock(clock)
        while done < n and done + half - 1 <= clock:
            if done == n - 1:
                collect(d_own, d_recv, d_ss, d_rs)
                for j in range(n):
                    din_ref[:, cols(j)] = d_recv[j]
            gradient(n - 1 - done)
            done += 1
    collect(g_send, g_recv, g_ss, g_rs)
    for j in range(n):
        grad_ref[:, cols(j)] = g_recv[j, :depth, :].astype(F32)
        dg_ref[:, cols(j)] = g_recv[j, depth : depth + PAD, :][0:1].astype(F32)
    for copy in pending + nq_copies:
        copy.wait_send()
    for layer in range(n):
        w_spread.drain(layer)
        q_spread.drain(layer)

        @pl.when(me != layer)
        def _():
            to_layer(d_own, d_recv, d_ss, d_rs, layer).wait_send()
            to_layer(g_send, g_recv, g_ss, g_rs, layer).wait_send()


def cascade(n, nd, micro, x_enc, x_dec, d_last, payload):
    rows, features = x_enc.shape
    width, depth, half = features // n, features // nd, nd // 2
    vmem = pl.BlockSpec(memory_space=pltpu.VMEM)
    sds = jax.ShapeDtypeStruct
    dma = pltpu.SemaphoreType.DMA
    return pl.pallas_call(
        functools.partial(cascade_kernel, n, nd, micro),
        out_shape=(
            sds((rows, features), BF16),
            sds((rows, features), BF16),
            sds((depth, features), F32),
            sds((1, features), F32),
        ),
        in_specs=[vmem] * 4,
        out_specs=[vmem] * 4,
        scratch_shapes=[
            pltpu.VMEM((n, nd, depth + PAD, width), BF16),
            pltpu.VMEM((n, nd, rows + PAD, width), BF16),
            pltpu.VMEM((n, nd, rows, depth), BF16),
            pltpu.VMEM((n, nd, rows, depth), BF16),
            pltpu.VMEM((n, n, PAD, width), BF16),
            pltpu.VMEM((n, n, rows, width), BF16),
            pltpu.VMEM((n, rows, width), BF16),
            pltpu.VMEM((n, n, rows, width + TAIL), BF16),
            pltpu.VMEM((n, n, rows, width + TAIL), BF16),
            pltpu.VMEM((n, rows, width), BF16),
            pltpu.VMEM((n, rows, width), BF16),
            pltpu.VMEM((n, rows, width), BF16),
            pltpu.VMEM((n, depth + PAD, width), BF16),
            pltpu.VMEM((n, depth + PAD, width), BF16),
            dma((n, n - 1)), dma((n, n - 1)),
            dma((n, n - 1)), dma((n, n - 1)),
            dma((n,)), dma((n,)),
            dma((n,)), dma((n,)),
            dma((n - 1,)), dma((n,)),
            dma((n, nd - 1)), dma((n, nd - 1)),
        ]
        + [
            dma((2, n, half)), dma((2, n, half)),
            dma((n, 2 * half)), dma((n, 2 * half)),
        ] * 2,
        compiler_params=pltpu.CompilerParams(
            collective_id=0, has_side_effects=True, vmem_limit_bytes=56 * 1024 * 1024
        ),
    )(x_enc, x_dec, d_last, payload)


def shards(x_enc, x_dec, d_out, lengths, w_query, gain):
    n, nd = lax.axis_size("section"), lax.axis_size("dp")
    micro, seq, features = x_enc.shape
    rows = micro * seq
    width, depth = features // n, features // nd
    row_index = lax.broadcasted_iota(jnp.int32, (micro, seq, 1), 1)
    d_last = jnp.where(row_index < lengths[:, :, None], d_out, jnp.zeros_like(d_out))
    split = w_query[0].reshape(depth, n, width).transpose(1, 0, 2)
    gain_rows = jnp.broadcast_to(jnp.pad(gain[0], (0, width - depth)), (n, PAD, width))
    payload = jnp.concatenate([split, gain_rows], axis=1)
    out, d_in, grad, gains = cascade(
        n, nd, micro, x_enc.reshape(rows, features), x_dec.reshape(rows, features),
        d_last.reshape(rows, features), payload,
    )
    gains = lax.dynamic_slice_in_dim(gains, lax.axis_index("dp") * depth, depth, axis=1)
    return (
        out.reshape(1, micro, seq, features),
        d_in.reshape(1, micro, seq, features),
        grad[None],
        gains,
    )


def solution(mesh):
    in_specs = (
        P(None, "dp", None), P(None, "dp", None), P(None, "dp", None),
        P(None, "dp"), P("section", "dp", None), P("section", "dp"),
    )
    out_specs = (
        P("section", None, "dp", None), P("section", None, "dp", None),
        P("section", "dp", None), P("section", "dp"),
    )
    return jax.shard_map(shards, mesh=mesh, in_specs=in_specs, out_specs=out_specs, check_vma=False)
```

```python
import functools

import jax
import jax.numpy as jnp
from jax import lax
from jax.experimental import pallas as pl
from jax.experimental.pallas import tpu as pltpu
from jax.sharding import PartitionSpec as P

HEAD = 256
norm_eps = 1e-06
mix_scale = 4.0
TAIL = 128
F32, BF16 = jnp.float32, jnp.bfloat16


def dot(left, right, left_dim, right_dim):
    return lax.dot_general(
        left, right, (((left_dim,), (right_dim,)), ((), ())), preferred_element_type=F32
    )


def inv_norm(chunks, features):
    total = sum(jnp.sum(c * c, axis=-1, keepdims=True) for c in chunks)
    return lax.rsqrt(total * (1.0 / features) + norm_eps)


def softmax_parts(query, keys):
    weights = jnp.exp(dot(query, keys, 1, 1) * HEAD ** (-0.5))
    return weights / jnp.sum(weights, axis=-1, keepdims=True)


MESH = pl.DeviceIdType.MESH
PAD = 16


class Spread:
    def __init__(self, buf, count, sems, paired):
        self.buf, self.count, self.paired = buf, count, paired
        self.chain_s, self.chain_r, self.pair_s, self.pair_r = sems
        here = lax.axis_index("dp")
        self.place, self.side = here // 2, lax.rem(here, 2)

    def copy(self, layer, place, side, send, recv, to_place, to_side):
        block = self.buf.at[layer, place * 2 + side]
        return pltpu.make_async_remote_copy(
            src_ref=block, dst_ref=block, send_sem=send, recv_sem=recv,
            device_id={"dp": to_place * 2 + to_side}, device_id_type=MESH,
        )

    def chain(self, layer, step, way):
        sign = 1 if way == 0 else -1
        return self.copy(
            layer, self.place - sign * step, self.side,
            self.chain_s.at[way, layer, step], self.chain_r.at[way, layer, step],
            self.place + sign, self.side,
        )

    def pair(self, layer, step, way, side):
        sign = 1 if way == 0 else -1
        slot = step if way == 0 else self.count - 1 + step
        return self.copy(
            layer, self.place - sign * step, side,
            self.pair_s.at[layer, slot], self.pair_r.at[layer, slot], self.place, 1 - self.side,
        )

    def holds(self, step, way):
        return self.place >= step if way == 0 else self.place + step < self.count

    def passes(self, step, way):
        end = self.place + 1 < self.count if way == 0 else self.place >= 1
        return jnp.logical_and(self.holds(step, way), end)

    def arrived(self, layer, step, way):
        sign = 1 if way == 0 else -1
        return self.copy(
            layer, self.place - sign * step, self.side,
            self.chain_s.at[way, layer, step - 1], self.chain_r.at[way, layer, step - 1],
            self.place + sign, self.side,
        )

    def pump(self, layer, step):
        for way in (0, 1):
            if step > 0:
                @pl.when(self.holds(step, way))
                def _():
                    self.arrived(layer, step, way).wait_recv()

            if step < self.count - 1:
                @pl.when(self.passes(step, way))
                def _():
                    self.chain(layer, step, way).start()

            if not self.paired:
                continue
            if step == 0:
                if way == 0:
                    self.pair(layer, 0, 0, self.side).start()
            else:
                @pl.when(self.holds(step, way))
                def _():
                    self.pair(layer, step, way, self.side).start()

    def finish(self, layer):
        self.pair(layer, 0, 0, 1 - self.side).wait_recv()
        for step in range(1, self.count):
            for way in (0, 1):
                @pl.when(self.holds(step, way))
                def _():
                    self.pair(layer, step, way, 1 - self.side).wait_recv()

    def drain(self, layer):
        if self.paired:
            self.pair(layer, 0, 0, self.side).wait_send()
        for step in range(self.count):
            for way in (0, 1):
                if step < self.count - 1:
                    @pl.when(self.passes(step, way))
                    def _():
                        self.chain(layer, step, way).wait_send()

                if step > 0 and self.paired:
                    @pl.when(self.holds(step, way))
                    def _():
                        self.pair(layer, step, way, self.side).wait_send()


def cascade_kernel(
    n, nd, micro, x_enc, x_dec, d_last, payload,
    out_ref, din_ref, grad_ref, dg_ref,
    weights, dq_all, nq_own, nq_all, gain, y_buf, x_one, p_send, p_recv, d_own, d_recv, q_buf, g_send, g_recv, g_part, h_send, h_recv,
    y_ss, y_rs, p_ss, p_rs, d_ss, d_rs, g_ss, g_rs, a_ss, a_rs, n_ss, n_rs, h_ss, h_rs,
    wz_s, wz_r, wy_s, wy_r, qz_s, qz_r,
):
    rows, features = x_enc.shape
    seq = rows // micro
    width = features // n
    depth = features // nd
    share = width // depth
    half = nd // 2
    heads = width // HEAD
    me = lax.axis_index("section")
    here = lax.axis_index("dp")
    mine = pl.ds(pl.multiple_of(me * width, width), width)
    peers = [lax.rem(me + k, n) for k in range(1, n)]
    behind = [lax.rem(me + n - k, n) for k in range(1, n)]
    place, side = here // 2, lax.rem(here, 2)
    places = [lax.rem(place + k, half) for k in range(1, half)]
    other = place * 2 + 1 - side
    dp_peers = [p * 2 + side for p in places] + [other]

    def cols(j):
        return slice(j * width, (j + 1) * width)

    barrier = pltpu.get_barrier_semaphore()
    for peer in peers:
        pl.semaphore_signal(barrier, inc=1, device_id={"section": peer}, device_id_type=MESH)
    for peer in dp_peers:
        pl.semaphore_signal(barrier, inc=1, device_id={"dp": peer}, device_id_type=MESH)
    pl.semaphore_wait(barrier, n - 1 + half)

    def describe(src, dst, send, recv, peer, axis="section"):
        return pltpu.make_async_remote_copy(
            src_ref=src, dst_ref=dst, send_sem=send, recv_sem=recv,
            device_id={axis: peer}, device_id_type=MESH,
        )

    def push(*args):
        copy = describe(*args)
        copy.start()
        return copy

    pending = []
    w_spread = Spread(weights, half, (wz_s, wz_r, wy_s, wy_r), True)
    q_spread = Spread(dq_all, half, (qz_s, qz_r, None, None), False)

    for k, peer in enumerate(peers):
        pending.append(
            push(payload.at[peer], weights.at[me, here], a_ss.at[k], a_rs.at[me], peer)
        )
    weights[me, here] = payload[me]

    def pump_weights(layer, step):
        if step == 0:
            @pl.when(me != layer)
            def _():
                describe(
                    payload.at[me], weights.at[layer, here], a_ss.at[0], a_rs.at[layer], peers[0]
                ).wait_recv()

        w_spread.pump(layer, step)

    def weight_clock(clock):
        for layer in range(n):
            if 0 <= clock - layer < half:
                pump_weights(layer, clock - layer)

    def layer_in(layer, j):
        if layer == 0:
            return x_enc[:, cols(j)].astype(F32)
        if layer == 1:
            return x_one[j].astype(F32)
        return y_buf[layer - 1, j].astype(F32)

    def own_in(layer):
        if layer == 0:
            return x_enc[:, mine]
        if layer == 1:
            return x_one[me]
        return y_buf[layer - 1, me]

    def own_source(layer):
        return x_enc[:, mine] if layer == 0 else y_buf[0, me]

    inv_in = [None] * n
    inv_src = [None] * n

    def gain_of(layer):
        return gain[layer, me][0:1].astype(F32)

    def keys_of(layer, source):
        return (source.astype(F32) * inv_src[layer] * gain_of(layer)).astype(BF16)

    for clock in range(half):
        weight_clock(clock)

    for layer in range(n):
        if layer == 1:
            for j in range(n):
                x_one[j] = (x_dec[:, cols(j)].astype(F32) + y_buf[0, j].astype(F32)).astype(BF16)
            inv_memory = inv_norm([y_buf[0, j].astype(F32) for j in range(n)], features)
        inv = inv_norm([layer_in(layer, j) for j in range(n)], features)
        inv_in[layer] = inv
        inv_src[layer] = inv if layer == 0 else inv_memory
        weight_clock(half + layer)
        w_spread.finish(layer)
        query = jnp.zeros((rows, width), F32)
        for j in range(n):
            scaled = layer_in(layer, j) * inv
            for i in range(share):
                b = j * share + i
                lanes = slice(i * depth, (i + 1) * depth)
                row = weights[layer, b, depth : depth + PAD, :depth]
                gain[layer, j, :, lanes] = row
                part = (scaled[:, lanes] * row[0:1].astype(F32)).astype(BF16)
                nq_own[layer, b] = part
                query = query + dot(part, weights[layer, b, :depth, :], 1, 0)
        query = query.astype(BF16)
        q_buf[layer] = query
        source = own_source(layer)
        keys = keys_of(layer, source)
        bands = []
        for m in range(micro):
            r = slice(m * seq, (m + 1) * seq)
            pieces = []
            for h in range(heads):
                c = slice(h * HEAD, (h + 1) * HEAD)
                probs = softmax_parts(query[r, c], keys[r, c]).astype(BF16)
                pieces.append(dot(probs, source[r, c], 1, 0))
            bands.append(jnp.concatenate(pieces, axis=1))
        mixed = jnp.concatenate(bands, axis=0).astype(BF16).astype(F32)
        y_buf[layer, me] = (own_in(layer).astype(F32) + mix_scale * mixed).astype(BF16)
        copies = [
            push(y_buf.at[layer, me], y_buf.at[layer, me], y_ss.at[layer, k], y_rs.at[layer, k], peer)
            for k, peer in enumerate(peers)
        ]
        if layer < n - 1:
            for copy in copies:
                copy.wait_recv()
        else:
            last = copies
        pending += copies

    nq_copies = []
    for layer in range(n - 1, -1, -1):
        for k, to in enumerate(places):
            nq_copies.append(
                push(
                    nq_own.at[layer, pl.ds(to * 2, 2)], nq_all.at[layer, place],
                    n_ss.at[layer, k], n_rs.at[layer, k], to * 2 + side, "dp",
                )
            )
        nq_all[layer, place] = nq_own[layer, pl.ds(place * 2, 2)]

    def query_clock(clock):
        for i in range(n):
            if 0 <= clock - i < half:
                q_spread.pump(n - 1 - i, clock - i)

    pair_copies = [
        describe(h_send.at[layer], h_recv.at[layer], h_ss.at[layer], h_rs.at[layer], other, "dp")
        for layer in range(n)
    ]

    def half_gradient(layer):
        i = n - 1 - layer
        for copy in nq_copies[i * (half - 1) : (i + 1) * (half - 1)]:
            copy.wait_recv()
        right = jnp.concatenate([dq_all[layer, c * 2 + side, :rows, :] for c in range(half)], axis=0)
        total = sum(dq_all[layer, c * 2 + side, rows:, :].astype(F32) for c in range(half))

        def product(to):
            left = jnp.concatenate([nq_all[layer, c, to] for c in range(half)], axis=0)
            return dot(left, right, 0, 0)

        h_send[layer, :depth, :] = product(1 - side).astype(BF16)
        h_send[layer, depth:, :] = total.astype(BF16)
        pair_copies[layer].start()
        g_part[layer, :depth, :] = product(side)
        g_part[layer, depth:, :] = total

    def whole_gradient(layer):
        pair_copies[layer].wait_recv()
        g_send[layer] = (g_part[layer] + h_recv[layer].astype(F32)).astype(BF16)
        deliver(g_send, g_recv, g_ss, g_rs, layer)

    def to_layer(buf, landing, send, recv, layer):
        return describe(buf.at[layer], landing.at[me], send.at[layer], recv.at[me], layer)

    def deliver(buf, landing, send, recv, layer):
        @pl.when(me != layer)
        def _():
            to_layer(buf, landing, send, recv, layer).start()

        @pl.when(me == layer)
        def _():
            landing[me] = buf[layer]

    def collect(buf, landing, send, recv):
        for b in behind:
            describe(buf.at[0], landing.at[b], send.at[0], recv.at[b], b).wait_recv()

    d_result = d_last[:, mine]
    d_memory = jnp.zeros((rows, width), F32)
    for layer in range(n - 1, -1, -1):
        g = gain_of(layer)
        source = own_source(layer)
        keys = keys_of(layer, source)
        query = q_buf[layer]
        d_mixed = (mix_scale * d_result.astype(F32)).astype(BF16)
        dq_bands, dk_bands, dv_bands = [], [], []
        for m in range(micro):
            r = slice(m * seq, (m + 1) * seq)
            dq_p, dk_p, dv_p = [], [], []
            for h in range(heads):
                c = slice(h * HEAD, (h + 1) * HEAD)
                probs = softmax_parts(query[r, c], keys[r, c])
                d_probs = dot(d_mixed[r, c], source[r, c], 1, 1).astype(BF16).astype(F32)
                dv_p.append(dot(probs.astype(BF16), d_mixed[r, c], 0, 0))
                inner = jnp.sum(d_probs * probs, axis=-1, keepdims=True)
                d_scores = (probs * (d_probs - inner) * HEAD ** (-0.5)).astype(BF16)
                dq_p.append(dot(d_scores, keys[r, c], 1, 0))
                dk_p.append(dot(d_scores, query[r, c], 0, 0))
            dq_bands.append(jnp.concatenate(dq_p, axis=1))
            dk_bands.append(jnp.concatenate(dk_p, axis=1))
            dv_bands.append(jnp.concatenate(dv_p, axis=1))
        d_query = jnp.concatenate(dq_bands, axis=0).astype(BF16)
        d_keys = jnp.concatenate(dk_bands, axis=0).astype(BF16).astype(F32)
        d_values = jnp.concatenate(dv_bands, axis=0).astype(BF16).astype(F32)
        q_sum = jnp.sum(d_query.astype(F32) * query.astype(F32), axis=-1, keepdims=True)
        k_sum = jnp.sum(d_keys * keys.astype(F32), axis=-1, keepdims=True)
        q_hi = q_sum.astype(BF16).astype(F32)
        k_hi = k_sum.astype(BF16).astype(F32)
        lane = lax.broadcasted_iota(jnp.int32, (rows, TAIL), 1)
        tail = jnp.where(
            lane == 0, q_hi, jnp.where(lane == 1, q_sum - q_hi, jnp.where(lane == 2, k_hi, k_sum - k_hi))
        ).astype(BF16)
        for b in range(nd):
            lanes = slice((b % share) * depth, (b % share + 1) * depth)
            p_send[layer, b // share, :, lanes] = dot(
                d_query, weights[layer, b, :depth, :], 1, 1
            ).astype(BF16)
        for j in range(n):
            p_send[layer, j, :, width:] = tail
        copies = [
            push(p_send.at[layer, peer], p_recv.at[layer, me], p_ss.at[layer, k], p_rs.at[layer, k], peer)
            for k, peer in enumerate(peers)
        ]
        for copy in copies:
            copy.wait_recv()
        pending += copies
        blocks = [p_send[layer, me]] + [p_recv[layer, b] for b in behind]
        d_normed = sum(b[:, :width].astype(F32) for b in blocks).astype(BF16).astype(F32)
        sums = sum(b[:, width:].astype(F32) for b in blocks)
        q_tot = sums[:, 0:1] + sums[:, 1:2]
        k_tot = sums[:, 2:3] + sums[:, 3:4]
        inv, inv_m = inv_in[layer], inv_src[layer]
        x_own = own_in(layer).astype(F32)
        s_own = source.astype(F32)
        d_input = d_result.astype(F32) + inv * (g * d_normed) - x_own * (inv * inv * q_tot * (1.0 / features))
        d_source = inv_m * (g * d_keys) - s_own * (inv_m * inv_m * k_tot * (1.0 / features)) + d_values
        gain_part = jnp.sum(x_own * inv * d_normed + s_own * inv_m * d_keys, axis=0, keepdims=True)
        dq_all[layer, here, :rows, :] = d_query
        dq_all[layer, here, rows:, :] = jnp.broadcast_to(gain_part, (PAD, width)).astype(BF16)
        query_clock(n - 1 - layer)
        if layer == 0:
            d_own[0] = (d_input + d_source).astype(BF16)
        else:
            d_result = d_input.astype(BF16)
            d_own[layer] = d_result
            d_memory = d_memory + d_source
            if layer == 1:
                d_result = (d_memory + d_result.astype(F32)).astype(BF16)
        deliver(d_own, d_recv, d_ss, d_rs, layer)

    for copy in last:
        copy.wait_recv()
    for j in range(n):
        out_ref[:, cols(j)] = y_buf[me, j]
    done = 0
    for clock in range(n, n + half):
        query_clock(clock)
        while done < n and done + half - 1 <= clock:
            half_gradient(n - 1 - done)
            if done > 0:
                whole_gradient(n - done)
            done += 1
    collect(d_own, d_recv, d_ss, d_rs)
    for j in range(n):
        din_ref[:, cols(j)] = d_recv[j]
    whole_gradient(0)
    collect(g_send, g_recv, g_ss, g_rs)
    for j in range(n):
        grad_ref[:, cols(j)] = g_recv[j, :depth, :].astype(F32)
        dg_ref[:, cols(j)] = g_recv[j, depth : depth + PAD, :][0:1].astype(F32)
    for copy in pending + nq_copies + pair_copies:
        copy.wait_send()
    for layer in range(n):
        w_spread.drain(layer)
        q_spread.drain(layer)

        @pl.when(me != layer)
        def _():
            to_layer(d_own, d_recv, d_ss, d_rs, layer).wait_send()
            to_layer(g_send, g_recv, g_ss, g_rs, layer).wait_send()


def cascade(n, nd, micro, x_enc, x_dec, d_last, payload):
    rows, features = x_enc.shape
    width, depth, half = features // n, features // nd, nd // 2
    vmem = pl.BlockSpec(memory_space=pltpu.VMEM)
    sds = jax.ShapeDtypeStruct
    dma = pltpu.SemaphoreType.DMA
    return pl.pallas_call(
        functools.partial(cascade_kernel, n, nd, micro),
        out_shape=(
            sds((rows, features), BF16),
            sds((rows, features), BF16),
            sds((depth, features), F32),
            sds((1, features), F32),
        ),
        in_specs=[vmem] * 4,
        out_specs=[vmem] * 4,
        scratch_shapes=[
            pltpu.VMEM((n, nd, depth + PAD, width), BF16),
            pltpu.VMEM((n, nd, rows + PAD, width), BF16),
            pltpu.VMEM((n, nd, rows, depth), BF16),
            pltpu.VMEM((n, half, 2, rows, depth), BF16),
            pltpu.VMEM((n, n, PAD, width), BF16),
            pltpu.VMEM((n, n, rows, width), BF16),
            pltpu.VMEM((n, rows, width), BF16),
            pltpu.VMEM((n, n, rows, width + TAIL), BF16),
            pltpu.VMEM((n, n, rows, width + TAIL), BF16),
            pltpu.VMEM((n, rows, width), BF16),
            pltpu.VMEM((n, rows, width), BF16),
            pltpu.VMEM((n, rows, width), BF16),
            pltpu.VMEM((n, depth + PAD, width), BF16),
            pltpu.VMEM((n, depth + PAD, width), BF16),
            pltpu.VMEM((n, depth + PAD, width), F32),
            pltpu.VMEM((n, depth + PAD, width), BF16),
            pltpu.VMEM((n, depth + PAD, width), BF16),
            dma((n, n - 1)), dma((n, n - 1)),
            dma((n, n - 1)), dma((n, n - 1)),
            dma((n,)), dma((n,)),
            dma((n,)), dma((n,)),
            dma((n - 1,)), dma((n,)),
            dma((n, half - 1)), dma((n, half - 1)),
            dma((n,)), dma((n,)),
            dma((2, n, half)), dma((2, n, half)),
            dma((n, 2 * half)), dma((n, 2 * half)),
            dma((2, n, half)), dma((2, n, half)),
        ],
        compiler_params=pltpu.CompilerParams(
            collective_id=0, has_side_effects=True, vmem_limit_bytes=56 * 1024 * 1024
        ),
    )(x_enc, x_dec, d_last, payload)


def shards(x_enc, x_dec, d_out, lengths, w_query, gain):
    n, nd = lax.axis_size("section"), lax.axis_size("dp")
    micro, seq, features = x_enc.shape
    rows = micro * seq
    width, depth = features // n, features // nd
    row_index = lax.broadcasted_iota(jnp.int32, (micro, seq, 1), 1)
    d_last = jnp.where(row_index < lengths[:, :, None], d_out, jnp.zeros_like(d_out))
    split = w_query[0].reshape(depth, n, width).transpose(1, 0, 2)
    gain_rows = jnp.broadcast_to(jnp.pad(gain[0], (0, width - depth)), (n, PAD, width))
    payload = jnp.concatenate([split, gain_rows], axis=1)
    out, d_in, grad, gains = cascade(
        n, nd, micro, x_enc.reshape(rows, features), x_dec.reshape(rows, features),
        d_last.reshape(rows, features), payload,
    )
    gains = lax.dynamic_slice_in_dim(gains, lax.axis_index("dp") * depth, depth, axis=1)
    return (
        out.reshape(1, micro, seq, features),
        d_in.reshape(1, micro, seq, features),
        grad[None],
        gains,
    )


def solution(mesh):
    in_specs = (
        P(None, "dp", None), P(None, "dp", None), P(None, "dp", None),
        P(None, "dp"), P("section", "dp", None), P("section", "dp"),
    )
    out_specs = (
        P("section", None, "dp", None), P("section", None, "dp", None),
        P("section", "dp", None), P("section", "dp"),
    )
    return jax.shard_map(shards, mesh=mesh, in_specs=in_specs, out_specs=out_specs, check_vma=False)
```

```python
import functools

import jax
import jax.numpy as jnp
from jax import lax
from jax.experimental import pallas as pl
from jax.experimental.pallas import tpu as pltpu
from jax.sharding import PartitionSpec as P

HEAD = 256
norm_eps = 1e-06
mix_scale = 4.0
TAIL = 128
F32, BF16 = jnp.float32, jnp.bfloat16


def dot(left, right, left_dim, right_dim):
    return lax.dot_general(
        left, right, (((left_dim,), (right_dim,)), ((), ())), preferred_element_type=F32
    )


def inv_norm(chunks, features):
    total = sum(jnp.sum(c * c, axis=-1, keepdims=True) for c in chunks)
    return lax.rsqrt(total * (1.0 / features) + norm_eps)


def softmax_parts(query, keys):
    weights = jnp.exp(dot(query, keys, 1, 1) * HEAD ** (-0.5))
    return weights / jnp.sum(weights, axis=-1, keepdims=True)


MESH = pl.DeviceIdType.MESH
PAD = 16


class Spread:
    def __init__(self, buf, count, sems):
        self.buf, self.count = buf, count
        self.chain_s, self.chain_r, self.pair_s, self.pair_r = sems
        here = lax.axis_index("dp")
        self.place, self.side = here // 2, lax.rem(here, 2)

    def copy(self, layer, place, side, send, recv, to_place, to_side):
        block = self.buf.at[layer, place * 2 + side]
        return pltpu.make_async_remote_copy(
            src_ref=block, dst_ref=block, send_sem=send, recv_sem=recv,
            device_id={"dp": to_place * 2 + to_side}, device_id_type=MESH,
        )

    def chain(self, layer, step, way):
        sign = 1 if way == 0 else -1
        return self.copy(
            layer, self.place - sign * step, self.side,
            self.chain_s.at[way, layer, step], self.chain_r.at[way, layer, step],
            self.place + sign, self.side,
        )

    def pair(self, layer, step, way, side):
        sign = 1 if way == 0 else -1
        slot = step if way == 0 else self.count - 1 + step
        return self.copy(
            layer, self.place - sign * step, side,
            self.pair_s.at[layer, slot], self.pair_r.at[layer, slot], self.place, 1 - self.side,
        )

    def holds(self, step, way):
        return self.place >= step if way == 0 else self.place + step < self.count

    def passes(self, step, way):
        end = self.place + 1 < self.count if way == 0 else self.place >= 1
        return jnp.logical_and(self.holds(step, way), end)

    def arrived(self, layer, step, way):
        sign = 1 if way == 0 else -1
        return self.copy(
            layer, self.place - sign * step, self.side,
            self.chain_s.at[way, layer, step - 1], self.chain_r.at[way, layer, step - 1],
            self.place + sign, self.side,
        )

    def pump(self, layer, step):
        for way in (0, 1):
            if step > 0:
                @pl.when(self.holds(step, way))
                def _():
                    self.arrived(layer, step, way).wait_recv()

            if step < self.count - 1:
                @pl.when(self.passes(step, way))
                def _():
                    self.chain(layer, step, way).start()

            if step == 0:
                if way == 0:
                    self.pair(layer, 0, 0, self.side).start()
            else:
                @pl.when(self.holds(step, way))
                def _():
                    self.pair(layer, step, way, self.side).start()

    def finish(self, layer):
        self.pair(layer, 0, 0, 1 - self.side).wait_recv()
        for step in range(1, self.count):
            for way in (0, 1):
                @pl.when(self.holds(step, way))
                def _():
                    self.pair(layer, step, way, 1 - self.side).wait_recv()

    def drain(self, layer):
        self.pair(layer, 0, 0, self.side).wait_send()
        for step in range(self.count):
            for way in (0, 1):
                if step < self.count - 1:
                    @pl.when(self.passes(step, way))
                    def _():
                        self.chain(layer, step, way).wait_send()

                if step > 0:
                    @pl.when(self.holds(step, way))
                    def _():
                        self.pair(layer, step, way, self.side).wait_send()


def cascade_kernel(
    n, nd, micro, x_enc, x_dec, d_last, payload,
    out_ref, din_ref, grad_ref, dg_ref,
    weights, dq_all, nq_own, nq_all, gain, y_buf, x_one, p_send, p_recv, d_own, d_recv, q_buf, g_send, g_recv,
    y_ss, y_rs, p_ss, p_rs, d_ss, d_rs, g_ss, g_rs, a_ss, a_rs, n_ss, n_rs,
    wz_s, wz_r, wy_s, wy_r, qz_s, qz_r, qy_s, qy_r,
):
    rows, features = x_enc.shape
    seq = rows // micro
    width = features // n
    depth = features // nd
    share = width // depth
    half = nd // 2
    heads = width // HEAD
    me = lax.axis_index("section")
    here = lax.axis_index("dp")
    mine = pl.ds(pl.multiple_of(me * width, width), width)
    peers = [lax.rem(me + k, n) for k in range(1, n)]
    behind = [lax.rem(me + n - k, n) for k in range(1, n)]
    dp_peers = [lax.rem(here + k, nd) for k in range(1, nd)]

    def cols(j):
        return slice(j * width, (j + 1) * width)

    barrier = pltpu.get_barrier_semaphore()
    for peer in peers:
        pl.semaphore_signal(barrier, inc=1, device_id={"section": peer}, device_id_type=MESH)
    for peer in dp_peers:
        pl.semaphore_signal(barrier, inc=1, device_id={"dp": peer}, device_id_type=MESH)
    pl.semaphore_wait(barrier, n - 1 + nd - 1)

    def describe(src, dst, send, recv, peer, axis="section"):
        return pltpu.make_async_remote_copy(
            src_ref=src, dst_ref=dst, send_sem=send, recv_sem=recv,
            device_id={axis: peer}, device_id_type=MESH,
        )

    def push(*args):
        copy = describe(*args)
        copy.start()
        return copy

    pending = []
    w_spread = Spread(weights, half, (wz_s, wz_r, wy_s, wy_r))
    q_spread = Spread(dq_all, half, (qz_s, qz_r, qy_s, qy_r))

    for k, peer in enumerate(peers):
        pending.append(
            push(payload.at[peer], weights.at[me, here], a_ss.at[k], a_rs.at[me], peer)
        )
    weights[me, here] = payload[me]

    def pump_weights(layer, step):
        if step == 0:
            @pl.when(me != layer)
            def _():
                describe(
                    payload.at[me], weights.at[layer, here], a_ss.at[0], a_rs.at[layer], peers[0]
                ).wait_recv()

        w_spread.pump(layer, step)

    def weight_clock(clock):
        for layer in range(n):
            if 0 <= clock - layer < half:
                pump_weights(layer, clock - layer)

    def layer_in(layer, j):
        if layer == 0:
            return x_enc[:, cols(j)].astype(F32)
        if layer == 1:
            return x_one[j].astype(F32)
        return y_buf[layer - 1, j].astype(F32)

    def own_in(layer):
        if layer == 0:
            return x_enc[:, mine]
        if layer == 1:
            return x_one[me]
        return y_buf[layer - 1, me]

    def own_source(layer):
        return x_enc[:, mine] if layer == 0 else y_buf[0, me]

    nq_copies = [None] * n
    inv_in = [None] * n
    inv_src = [None] * n

    def gain_of(layer):
        return gain[layer, me][0:1].astype(F32)

    def keys_of(layer, source):
        return (source.astype(F32) * inv_src[layer] * gain_of(layer)).astype(BF16)

    for clock in range(half):
        weight_clock(clock)

    for layer in range(n):
        if layer == 1:
            for j in range(n):
                x_one[j] = (x_dec[:, cols(j)].astype(F32) + y_buf[0, j].astype(F32)).astype(BF16)
            inv_memory = inv_norm([y_buf[0, j].astype(F32) for j in range(n)], features)
        inv = inv_norm([layer_in(layer, j) for j in range(n)], features)
        inv_in[layer] = inv
        inv_src[layer] = inv if layer == 0 else inv_memory
        weight_clock(half + layer)
        w_spread.finish(layer)
        query = jnp.zeros((rows, width), F32)
        for j in range(n):
            scaled = layer_in(layer, j) * inv
            for i in range(share):
                b = j * share + i
                lanes = slice(i * depth, (i + 1) * depth)
                row = weights[layer, b, depth : depth + PAD, :depth]
                gain[layer, j, :, lanes] = row
                part = (scaled[:, lanes] * row[0:1].astype(F32)).astype(BF16)
                nq_own[layer, b] = part
                query = query + dot(part, weights[layer, b, :depth, :], 1, 0)
        query = query.astype(BF16)
        q_buf[layer] = query
        source = own_source(layer)
        keys = keys_of(layer, source)
        bands = []
        for m in range(micro):
            r = slice(m * seq, (m + 1) * seq)
            pieces = []
            for h in range(heads):
                c = slice(h * HEAD, (h + 1) * HEAD)
                probs = softmax_parts(query[r, c], keys[r, c]).astype(BF16)
                pieces.append(dot(probs, source[r, c], 1, 0))
            bands.append(jnp.concatenate(pieces, axis=1))
        mixed = jnp.concatenate(bands, axis=0).astype(BF16).astype(F32)
        y_buf[layer, me] = (own_in(layer).astype(F32) + mix_scale * mixed).astype(BF16)
        copies = [
            push(y_buf.at[layer, me], y_buf.at[layer, me], y_ss.at[layer, k], y_rs.at[layer, k], peer)
            for k, peer in enumerate(peers)
        ]
        nq_copies[layer] = [
            push(
                nq_own.at[layer, peer], nq_all.at[layer, here],
                n_ss.at[layer, k], n_rs.at[layer, k], peer, "dp",
            )
            for k, peer in enumerate(dp_peers)
        ]
        nq_all[layer, here] = nq_own[layer, here]
        if layer < n - 1:
            for copy in copies:
                copy.wait_recv()
        else:
            last = copies
        pending += copies

    def query_clock(clock):
        for i in range(n):
            if 0 <= clock - i < half:
                q_spread.pump(n - 1 - i, clock - i)

    def gradient(layer):
        q_spread.finish(layer)
        for copy in nq_copies[layer]:
            copy.wait_recv()
        left = nq_all[layer].reshape(nd * rows, depth)
        right = jnp.concatenate([dq_all[layer, b, :rows, :] for b in range(nd)], axis=0)
        g_send[layer, :depth, :] = dot(left, right, 0, 0).astype(BF16)
        total = sum(dq_all[layer, b, rows : rows + PAD, :].astype(F32) for b in range(nd))
        g_send[layer, depth:, :] = total.astype(BF16)
        deliver(g_send, g_recv, g_ss, g_rs, layer)

    def to_layer(buf, landing, send, recv, layer):
        return describe(buf.at[layer], landing.at[me], send.at[layer], recv.at[me], layer)

    def deliver(buf, landing, send, recv, layer):
        @pl.when(me != layer)
        def _():
            to_layer(buf, landing, send, recv, layer).start()

        @pl.when(me == layer)
        def _():
            landing[me] = buf[layer]

    def collect(buf, landing, send, recv):
        for b in behind:
            describe(buf.at[0], landing.at[b], send.at[0], recv.at[b], b).wait_recv()

    d_result = d_last[:, mine]
    d_memory = jnp.zeros((rows, width), F32)
    for layer in range(n - 1, -1, -1):
        g = gain_of(layer)
        source = own_source(layer)
        keys = keys_of(layer, source)
        query = q_buf[layer]
        d_mixed = (mix_scale * d_result.astype(F32)).astype(BF16)
        dq_bands, dk_bands, dv_bands = [], [], []
        for m in range(micro):
            r = slice(m * seq, (m + 1) * seq)
            dq_p, dk_p, dv_p = [], [], []
            for h in range(heads):
                c = slice(h * HEAD, (h + 1) * HEAD)
                probs = softmax_parts(query[r, c], keys[r, c])
                d_probs = dot(d_mixed[r, c], source[r, c], 1, 1).astype(BF16).astype(F32)
                dv_p.append(dot(probs.astype(BF16), d_mixed[r, c], 0, 0))
                inner = jnp.sum(d_probs * probs, axis=-1, keepdims=True)
                d_scores = (probs * (d_probs - inner) * HEAD ** (-0.5)).astype(BF16)
                dq_p.append(dot(d_scores, keys[r, c], 1, 0))
                dk_p.append(dot(d_scores, query[r, c], 0, 0))
            dq_bands.append(jnp.concatenate(dq_p, axis=1))
            dk_bands.append(jnp.concatenate(dk_p, axis=1))
            dv_bands.append(jnp.concatenate(dv_p, axis=1))
        d_query = jnp.concatenate(dq_bands, axis=0).astype(BF16)
        d_keys = jnp.concatenate(dk_bands, axis=0).astype(BF16).astype(F32)
        d_values = jnp.concatenate(dv_bands, axis=0).astype(BF16).astype(F32)
        q_sum = jnp.sum(d_query.astype(F32) * query.astype(F32), axis=-1, keepdims=True)
        k_sum = jnp.sum(d_keys * keys.astype(F32), axis=-1, keepdims=True)
        q_hi = q_sum.astype(BF16).astype(F32)
        k_hi = k_sum.astype(BF16).astype(F32)
        lane = lax.broadcasted_iota(jnp.int32, (rows, TAIL), 1)
        tail = jnp.where(
            lane == 0, q_hi, jnp.where(lane == 1, q_sum - q_hi, jnp.where(lane == 2, k_hi, k_sum - k_hi))
        ).astype(BF16)
        for b in range(nd):
            lanes = slice((b % share) * depth, (b % share + 1) * depth)
            p_send[layer, b // share, :, lanes] = dot(
                d_query, weights[layer, b, :depth, :], 1, 1
            ).astype(BF16)
        for j in range(n):
            p_send[layer, j, :, width:] = tail
        copies = [
            push(p_send.at[layer, peer], p_recv.at[layer, me], p_ss.at[layer, k], p_rs.at[layer, k], peer)
            for k, peer in enumerate(peers)
        ]
        for copy in copies:
            copy.wait_recv()
        pending += copies
        blocks = [p_send[layer, me]] + [p_recv[layer, b] for b in behind]
        d_normed = sum(b[:, :width].astype(F32) for b in blocks).astype(BF16).astype(F32)
        sums = sum(b[:, width:].astype(F32) for b in blocks)
        q_tot = sums[:, 0:1] + sums[:, 1:2]
        k_tot = sums[:, 2:3] + sums[:, 3:4]
        inv, inv_m = inv_in[layer], inv_src[layer]
        x_own = own_in(layer).astype(F32)
        s_own = source.astype(F32)
        d_input = d_result.astype(F32) + inv * (g * d_normed) - x_own * (inv * inv * q_tot * (1.0 / features))
        d_source = inv_m * (g * d_keys) - s_own * (inv_m * inv_m * k_tot * (1.0 / features)) + d_values
        gain_part = jnp.sum(x_own * inv * d_normed + s_own * inv_m * d_keys, axis=0, keepdims=True)
        dq_all[layer, here, :rows, :] = d_query
        dq_all[layer, here, rows:, :] = jnp.broadcast_to(gain_part, (PAD, width)).astype(BF16)
        query_clock(n - 1 - layer)
        if layer == 0:
            d_own[0] = (d_input + d_source).astype(BF16)
        else:
            d_result = d_input.astype(BF16)
            d_own[layer] = d_result
            d_memory = d_memory + d_source
            if layer == 1:
                d_result = (d_memory + d_result.astype(F32)).astype(BF16)
        deliver(d_own, d_recv, d_ss, d_rs, layer)

    for copy in last:
        copy.wait_recv()
    for j in range(n):
        out_ref[:, cols(j)] = y_buf[me, j]
    done = 0
    for clock in range(n, n + half):
        query_clock(clock)
        while done < n and done + half - 1 <= clock:
            if done == n - 1:
                collect(d_own, d_recv, d_ss, d_rs)
                for j in range(n):
                    din_ref[:, cols(j)] = d_recv[j]
            gradient(n - 1 - done)
            done += 1
    collect(g_send, g_recv, g_ss, g_rs)
    for j in range(n):
        grad_ref[:, cols(j)] = g_recv[j, :depth, :].astype(F32)
        dg_ref[:, cols(j)] = g_recv[j, depth : depth + PAD, :][0:1].astype(F32)
    for copy in pending + sum(nq_copies, []):
        copy.wait_send()
    for layer in range(n):
        w_spread.drain(layer)
        q_spread.drain(layer)

        @pl.when(me != layer)
        def _():
            to_layer(d_own, d_recv, d_ss, d_rs, layer).wait_send()
            to_layer(g_send, g_recv, g_ss, g_rs, layer).wait_send()


def cascade(n, nd, micro, x_enc, x_dec, d_last, payload):
    rows, features = x_enc.shape
    width, depth, half = features // n, features // nd, nd // 2
    vmem = pl.BlockSpec(memory_space=pltpu.VMEM)
    sds = jax.ShapeDtypeStruct
    dma = pltpu.SemaphoreType.DMA
    return pl.pallas_call(
        functools.partial(cascade_kernel, n, nd, micro),
        out_shape=(
            sds((rows, features), BF16),
            sds((rows, features), BF16),
            sds((depth, features), F32),
            sds((1, features), F32),
        ),
        in_specs=[vmem] * 4,
        out_specs=[vmem] * 4,
        scratch_shapes=[
            pltpu.VMEM((n, nd, depth + PAD, width), BF16),
            pltpu.VMEM((n, nd, rows + PAD, width), BF16),
            pltpu.VMEM((n, nd, rows, depth), BF16),
            pltpu.VMEM((n, nd, rows, depth), BF16),
            pltpu.VMEM((n, n, PAD, width), BF16),
            pltpu.VMEM((n, n, rows, width), BF16),
            pltpu.VMEM((n, rows, width), BF16),
            pltpu.VMEM((n, n, rows, width + TAIL), BF16),
            pltpu.VMEM((n, n, rows, width + TAIL), BF16),
            pltpu.VMEM((n, rows, width), BF16),
            pltpu.VMEM((n, rows, width), BF16),
            pltpu.VMEM((n, rows, width), BF16),
            pltpu.VMEM((n, depth + PAD, width), BF16),
            pltpu.VMEM((n, depth + PAD, width), BF16),
            dma((n, n - 1)), dma((n, n - 1)),
            dma((n, n - 1)), dma((n, n - 1)),
            dma((n,)), dma((n,)),
            dma((n,)), dma((n,)),
            dma((n - 1,)), dma((n,)),
            dma((n, nd - 1)), dma((n, nd - 1)),
        ]
        + [
            dma((2, n, half)), dma((2, n, half)),
            dma((n, 2 * half)), dma((n, 2 * half)),
        ] * 2,
        compiler_params=pltpu.CompilerParams(
            collective_id=0, has_side_effects=True, vmem_limit_bytes=56 * 1024 * 1024
        ),
    )(x_enc, x_dec, d_last, payload)


def shards(x_enc, x_dec, d_out, lengths, w_query, gain):
    n, nd = lax.axis_size("section"), lax.axis_size("dp")
    micro, seq, features = x_enc.shape
    rows = micro * seq
    width, depth = features // n, features // nd
    row_index = lax.broadcasted_iota(jnp.int32, (micro, seq, 1), 1)
    d_last = jnp.where(row_index < lengths[:, :, None], d_out, jnp.zeros_like(d_out))
    split = w_query[0].reshape(depth, n, width).transpose(1, 0, 2)
    gain_rows = jnp.broadcast_to(jnp.pad(gain[0], (0, width - depth)), (n, PAD, width))
    payload = jnp.concatenate([split, gain_rows], axis=1)
    out, d_in, grad, gains = cascade(
        n, nd, micro, x_enc.reshape(rows, features), x_dec.reshape(rows, features),
        d_last.reshape(rows, features), payload,
    )
    gains = lax.dynamic_slice_in_dim(gains, lax.axis_index("dp") * depth, depth, axis=1)
    return (
        out.reshape(1, micro, seq, features),
        d_in.reshape(1, micro, seq, features),
        grad[None],
        gains,
    )


def solution(mesh):
    in_specs = (
        P(None, "dp", None), P(None, "dp", None), P(None, "dp", None),
        P(None, "dp"), P("section", "dp", None), P("section", "dp"),
    )
    out_specs = (
        P("section", None, "dp", None), P("section", None, "dp", None),
        P("section", "dp", None), P("section", "dp"),
    )
    return jax.shard_map(shards, mesh=mesh, in_specs=in_specs, out_specs=out_specs, check_vma=False)
```
